32 devices in a mesh: groups: 2 (over y), replica: 4 (over x, core), tensor: 4 (over z).
Axes of the slice: x: 2, y: 2, z: 4, core: 2. Of those that a mesh axis runs over, the one named last changes fastest.
Arguments:
- queries: bfloat16 [4096, 8192], P(('groups', 'replica', 'tensor')), parts along dimension 0, may hold values from -28 to 28
- keys: bfloat16 [4096, 32, 1024], P(('groups', 'replica', 'tensor')), parts along dimension 0, may hold values from -6 to 6
- values: bfloat16 [4096, 32, 1024], P(('groups', 'replica', 'tensor')), parts along dimension 0, may hold values from -6 to 6
- lengths: int32 [4096], P(('groups', 'replica', 'tensor')), parts along dimension 0, may hold values from 2 to 32, as said below
- output_projection_weight: bfloat16 [8192, 4096], P(None, 'tensor'), may hold values from -0.0625 to 0.0625
- adapter_down_factors: bfloat16 [96, 8192, 64], P(('groups', 'replica'), 'tensor'), parts along dimension 0, may hold values from -0.0625 to 0.0625
- adapter_up_factors: bfloat16 [96, 64, 4096], P(('groups', 'replica'), None, 'tensor'), parts along dimension 0, may hold values from -0.75 to 0.75
- block_adapter_index: int32 [32], P(('groups', 'replica')), parts along dimension 0, may hold values from 0 to 47
- block_live_rows: int32 [32], P(('groups', 'replica')), parts along dimension 0, may hold values from 1 to 128, as said below
- adapter_storage_slot: int32 [96], P('groups'), parts along dimension 0, may hold values from 0 to 47, each once
Outputs:
- projected: bfloat16 [4096, 4096], P(('groups', 'replica'), 'tensor'), parts along dimension 0
The draws below stay inside these ranges and needn't reach their ends.
There are 2 independent parts, one for each index of `groups`. The reference program is written for one: setup_inputs(seed, part) draws one part's arguments, and reference() takes and returns one part's arrays. A program takes and returns all parts, laid end to end along the dimension named above; an argument that names none is the same for every part. Nothing has to cross between parts.
Inputs may be any that keep to these rules, and one draw needn't show every extreme that they name: `lengths`: some row has the full length 32. `block_live_rows`: the first block of each draw is full. Adapter a is stored at slot adapter_storage_slot[a], on replica adapter_storage_slot[a] // 12.
All inputs are finite; a program needn't handle non-finite values.
Results may differ from the reference program's by a relative error of at most 0.01.
Values may be sent and summed in bfloat16 or wider, within the bound.
No kernel may reach another device: no remote copies, remote signals or barrier semaphores. Data moves between devices by JAX's collectives and lax.ppermute only.
A program may use at most 192 MiB of HBM per device.

```python
import math
import jax
import jax.numpy as jnp
import numpy as np

QUERY_HEAD_COUNT = 64
KVH = 8
HEAD_SIZE = 128
OUTPUT_FEATURES = 4096
ADAPTER_RANK = 64
BLOCK = 128
LEN = 32
ROWS = 2048
ADAPTER_COUNT = 48


def cache_normal(key):
    drawn = jax.random.normal(jax.random.fold_in(key, 5), (ROWS, LEN, KVH * HEAD_SIZE), jnp.float32)
    return jnp.clip(drawn, -6.0, 6.0)


def aligned_heads(key):
    row_ids = jnp.arange(ROWS)
    head_ids = jnp.arange(QUERY_HEAD_COUNT)
    picked_rows = (jax.random.randint(jax.random.fold_in(key, 7), (ROWS,), 0, 8) == 0) | (row_ids == 0)
    picked_heads = jax.random.randint(jax.random.fold_in(key, 9), (ROWS, QUERY_HEAD_COUNT), 0, 2) == 0
    forced = (row_ids[:, None] == 0) & (head_ids[None, :] == 0)
    chosen = picked_rows[:, None] & (picked_heads | forced)
    levels = jax.random.randint(jax.random.fold_in(key, 13), (ROWS,), 2, 5)
    levels = jnp.where(row_ids == 0, 4, levels)
    return (chosen, picked_rows, 7.0 * levels.astype(jnp.float32))


def draw_keys(key, part):
    cache = cache_normal(key)
    chosen, picked_rows, strength = aligned_heads(key)
    second = jnp.where(picked_rows[:, None], 0.99 * cache[:, 0], cache[:, 1])
    cache = cache.at[:, 1].set(second)
    return cache.astype(jnp.bfloat16)


def draw_queries(key, part):
    cache = cache_normal(key)
    chosen, picked_rows, strength = aligned_heads(key)
    key = jax.random.fold_in(key, 41)
    entries = jnp.clip(jax.random.normal(key, (ROWS, QUERY_HEAD_COUNT, HEAD_SIZE), jnp.float32), -6.0, 6.0)
    signs = jnp.sign(cache[:, 0]).reshape(ROWS, KVH, 1, HEAD_SIZE)
    signs = jnp.broadcast_to(signs, (ROWS, KVH, QUERY_HEAD_COUNT // KVH, HEAD_SIZE)).reshape(ROWS, QUERY_HEAD_COUNT, HEAD_SIZE)
    aligned = strength[:, None, None] * signs
    drawn = jnp.where(chosen[:, :, None], aligned, entries)
    return drawn.reshape(ROWS, QUERY_HEAD_COUNT * HEAD_SIZE).astype(jnp.bfloat16)


def draw_lengths(key, part):
    key = jax.random.fold_in(key, 11)
    drawn = jax.random.randint(key, (ROWS,), 2, LEN + 1)
    return drawn.at[0].set(LEN).astype(jnp.int32)


def draw_block_live_rows(key, part):
    key = jax.random.fold_in(key, 23)
    drawn = jax.random.randint(key, (ROWS // BLOCK,), 1, BLOCK + 1)
    return drawn.at[0].set(BLOCK).astype(jnp.int32)


def set_ends(result, stream_key, smallest, top_value):
    longest = result.shape.index(max(result.shape))
    spots = []
    for shift in (0, 1):
        where = [jax.random.randint(jax.random.fold_in(stream_key, axis), (), 0, length) for axis, length in enumerate(result.shape)]
        where[longest] = (where[longest] + shift) % result.shape[longest]
        spots.append(tuple(where))
    return result.at[spots[0]].set(smallest).at[spots[1]].set(top_value)


def block_levels(own_key, extent, pieces, low, top_value):
    loudness = 1.0
    for dim, parts in pieces:
        heights = jax.random.uniform(jax.random.fold_in(jax.random.fold_in(own_key, 6), dim), (parts,), jnp.float32, low / len(pieces), top_value / len(pieces))
        loudness = loudness * jnp.repeat(jnp.exp(heights), extent[dim] // parts).reshape((-1,) + (1,) * (len(extent) - 1 - dim))
    return loudness


def cumulative_ranks(amount, lean):
    weights = [(1 << 20) // math.isqrt(standing ** lean) + 1 for standing in range(1, amount + 1)]
    spread = 1 + sum(weights) // (1 << 30)
    return np.cumsum(np.array([max(1, weight // spread) for weight in weights]))


def ranked_ids(own_key, shape, number_of, skew):
    table = cumulative_ranks(number_of, skew)
    ticket = jax.random.randint(jax.random.fold_in(own_key, 1), shape, 0, int(table[number_of - 1]))
    grade = jnp.searchsorted(jnp.asarray(table, jnp.int32), ticket, side="right")
    return jax.random.permutation(jax.random.fold_in(own_key, 2), number_of)[grade].astype(jnp.int32)


def scatter_about(rng, dims, width, bound, pieces=(), kind=jnp.bfloat16):
    values = width * jax.random.normal(rng, dims, jnp.float32)
    if pieces:
        values = values * block_levels(rng, dims, pieces, -0.22, 0.18)
    return jnp.clip(values, -bound, bound).astype(kind)


def setup_inputs(seed: int = 0, part: int = 0) -> dict:
    key_list = jax.random.split(jax.random.key(seed), 11)
    part_splits = jax.random.split(jax.random.fold_in(key_list[10], part), 11)
    return {
        "queries": draw_queries(jax.random.fold_in(jax.random.fold_in(key_list[10], part), 71), part),
        "keys": draw_keys(jax.random.fold_in(jax.random.fold_in(key_list[10], part), 71), part),
        "values": scatter_about(part_splits[2], (ROWS, LEN, KVH * HEAD_SIZE), 1.0, 6.0, ((0, 16),)),
        "lengths": draw_lengths(jax.random.fold_in(jax.random.fold_in(key_list[10], part), 71), part),
        "output_projection_weight": scatter_about(key_list[4], (QUERY_HEAD_COUNT * HEAD_SIZE, OUTPUT_FEATURES), (QUERY_HEAD_COUNT * HEAD_SIZE) ** -0.5, 0.0625, ((1, 4),)),
        "adapter_down_factors": scatter_about(part_splits[5], (ADAPTER_COUNT, QUERY_HEAD_COUNT * HEAD_SIZE, ADAPTER_RANK), (QUERY_HEAD_COUNT * HEAD_SIZE) ** -0.5, 0.0625, ((0, 4), (1, 4))),
        "adapter_up_factors": scatter_about(part_splits[6], (ADAPTER_COUNT, ADAPTER_RANK, OUTPUT_FEATURES), ADAPTER_RANK ** -0.5, 0.75, ((0, 4), (2, 4))),
        "block_adapter_index": set_ends(ranked_ids(part_splits[7], (ROWS // BLOCK,), ADAPTER_COUNT, 2), jax.random.fold_in(part_splits[7], 3), 0, ADAPTER_COUNT - 1).astype(jnp.int32),
        "block_live_rows": draw_block_live_rows(jax.random.fold_in(jax.random.fold_in(key_list[10], part), 71), part),
        "adapter_storage_slot": jax.random.permutation(part_splits[9], ADAPTER_COUNT).astype(jnp.int32),
    }


def reference(queries, keys, values, lengths, output_projection_weight, adapter_down_factors, adapter_up_factors, block_adapter_index, block_live_rows, adapter_storage_slot):
    row_count = queries.shape[0]
    group_size = QUERY_HEAD_COUNT // KVH
    query_heads = queries.reshape(row_count, KVH, group_size, HEAD_SIZE).astype(jnp.float32)
    key_heads = keys.reshape(row_count, LEN, KVH, HEAD_SIZE).astype(jnp.float32)
    value_heads = values.reshape(row_count, LEN, KVH, HEAD_SIZE).astype(jnp.float32)
    scores = jnp.einsum("rkgd,rpkd->rkgp", query_heads, key_heads) * (HEAD_SIZE ** -0.5)
    visible = (jnp.arange(LEN)[None, :] < lengths[:, None])[:, None, None, :]
    scores = jnp.where(visible, scores, -1e30)
    highest = jnp.max(scores, axis=3, keepdims=True)
    weights = jnp.where(visible, jnp.exp(scores - highest), 0.0)
    totals = jnp.sum(weights, axis=3)
    summed = jnp.einsum("rkgp,rpkd->rkgd", weights, value_heads)
    attended = (summed / totals[..., None]).reshape(row_count, QUERY_HEAD_COUNT * HEAD_SIZE).astype(jnp.bfloat16)
    base = jnp.dot(attended, output_projection_weight, preferred_element_type=jnp.float32)
    storage_slots = adapter_storage_slot[block_adapter_index]
    selected_down_factor = adapter_down_factors[storage_slots].astype(jnp.float32)
    selected_up_factor = adapter_up_factors[storage_slots].astype(jnp.float32)
    blocked = attended.reshape(-1, BLOCK, QUERY_HEAD_COUNT * HEAD_SIZE).astype(jnp.float32)
    reduced = jnp.einsum("bri,bik->brk", blocked, selected_down_factor).astype(jnp.bfloat16)
    delta = jnp.einsum("brk,bkc->brc", reduced.astype(jnp.float32), selected_up_factor).reshape(row_count, OUTPUT_FEATURES)
    live = (jnp.arange(BLOCK)[None, :] < block_live_rows[:, None]).reshape(row_count)
    return jnp.where(live[:, None], base + 2.0 * delta, 0.0).astype(jnp.bfloat16)
```

```python
import functools

import jax
import jax.numpy as jnp
from jax import lax
from jax.experimental import pallas as pl
from jax.experimental.pallas import tpu as pltpu
from jax.sharding import PartitionSpec as P

QUERY_HEAD_COUNT = 64
KVH = 8
HEAD_SIZE = 128
LINE = 4
PARTS = 2
ANY = pl.BlockSpec(memory_space=pl.ANY)
SMEM = pl.BlockSpec(memory_space=pltpu.SMEM)
VMEM = pl.BlockSpec(memory_space=pltpu.VMEM)
BIG = pltpu.CompilerParams(vmem_limit_bytes=40 * 2**20)


def attention(queries, keys, values, lengths):
    row_count = queries.shape[0]
    span = keys.shape[1]
    group_size = QUERY_HEAD_COUNT // KVH
    query_heads = queries.reshape(row_count, KVH, group_size, HEAD_SIZE)
    key_heads = keys.reshape(row_count, span, KVH, HEAD_SIZE)
    value_heads = values.reshape(row_count, span, KVH, HEAD_SIZE).astype(jnp.float32)
    scores = jnp.einsum(
        "rkgd,rpkd->rkgp", query_heads, key_heads, preferred_element_type=jnp.float32
    ) * HEAD_SIZE ** (-0.5)
    visible = (jnp.arange(span)[None, :] < lengths[:, None])[:, None, None, :]
    scores = jnp.where(visible, scores, -1e30)
    highest = jnp.max(scores, axis=3, keepdims=True)
    weights = jnp.where(visible, jnp.exp(scores - highest), 0.0)
    totals = jnp.sum(weights, axis=3)
    summed = jnp.einsum("rkgp,rpkd->rkgd", weights, value_heads)
    return (
        (summed / totals[..., None])
        .reshape(row_count, QUERY_HEAD_COUNT * HEAD_SIZE)
        .astype(jnp.bfloat16)
    )


def slot_of(replicas, ids_ref, slots_ref, here, target, b):
    return slots_ref[ids_ref[lax.rem(target - here + replicas, replicas), b]]


def factor_copies(act, at, down_ref, up_ref, target, sems):
    depth = down_ref.shape[2]
    act(pltpu.make_async_copy(down_ref.at[at], target.at[:, pl.ds(0, depth)], sems.at[0]))
    act(pltpu.make_async_copy(up_ref.at[at], target.at[:, pl.ds(depth, up_ref.shape[2])], sems.at[1]))


def pair_kernel(replicas, blocks, here_ref, ids_ref, slots_ref, down_ref, up_ref, out_ref, sems):
    own = down_ref.shape[0]
    pairs = replicas // 2
    here = here_ref[0]
    pair, core = lax.div(here, 2), lax.rem(here, 2)

    def each(act):
        for k in range(pairs):
            target = lax.rem(pair + k, pairs) * 2 + 1 - core
            for b in range(blocks):
                slot = slot_of(replicas, ids_ref, slots_ref, here, target, b)

                @pl.when(lax.div(slot, own) == here)
                def _():
                    factor_copies(
                        act, lax.rem(slot, own), down_ref, up_ref, out_ref.at[k, b], sems.at[k, b]
                    )

    each(lambda copy: copy.start())
    each(lambda copy: copy.wait())


def merge_kernel(
    replicas, blocks, here_ref, ids_ref, slots_ref, down_ref, up_ref, paired_ref, out_ref, sems
):
    own = down_ref.shape[0]
    pairs = replicas // 2
    here = here_ref[0]
    pair, core = lax.div(here, 2), lax.rem(here, 2)

    def each(act):
        for k in range(1, pairs):
            target = lax.rem(pair + k, pairs) * 2 + core
            for b in range(blocks):
                slot = slot_of(replicas, ids_ref, slots_ref, here, target, b)
                home = lax.div(slot, own)
                place = out_ref.at[k - 1, b]

                @pl.when(home == here)
                def _():
                    factor_copies(
                        act, lax.rem(slot, own), down_ref, up_ref, place, sems.at[k - 1, b]
                    )

                @pl.when(home == pair * 2 + 1 - core)
                def _():
                    act(pltpu.make_async_copy(paired_ref.at[k, b], place, sems.at[k - 1, b, 0]))

    each(lambda copy: copy.start())
    each(lambda copy: copy.wait())


def pick_kernel(
    replicas,
    blocks,
    here_ref,
    ids_ref,
    slots_ref,
    order_ref,
    down_ref,
    up_ref,
    paired_ref,
    *refs,
):
    out_ref, sems = refs[-2:]
    fetched = refs[:-2]
    own = down_ref.shape[0]
    pairs = replicas // 2
    here = here_ref[0]
    pair = lax.div(here, 2)

    def each(act):
        for i in range(blocks):
            b = order_ref[i]
            slot = slots_ref[ids_ref[0, b]]
            home = lax.div(slot, own)
            shift = lax.rem(pair - lax.div(home, 2) + pairs, pairs)

            @pl.when(home == here)
            def _():
                factor_copies(act, lax.rem(slot, own), down_ref, up_ref, out_ref.at[i], sems.at[i])

            @pl.when((shift == 0) & (home != here))
            def _():
                act(pltpu.make_async_copy(paired_ref.at[0, b], out_ref.at[i], sems.at[i, 0]))

            for k in range(1, pairs):

                @pl.when(shift == k)
                def _():
                    act(pltpu.make_async_copy(fetched[k - 1].at[b], out_ref.at[i], sems.at[i, 0]))

    each(lambda copy: copy.start())
    each(lambda copy: copy.wait())


def pair_factors(down, up, ids, slots):
    replicas = lax.axis_size("replica")
    here = lax.axis_index("replica").astype(jnp.int32)[None]
    blocks = ids.shape[0]
    all_ids = jnp.stack(
        [ids]
        + [
            lax.ppermute(ids, "replica", [(i, (i - shift) % replicas) for i in range(replicas)])
            for shift in range(1, replicas)
        ]
    )
    pairs = replicas // 2
    piece = (blocks, down.shape[1], down.shape[2] + up.shape[2])
    packed = pl.pallas_call(
        functools.partial(pair_kernel, replicas, blocks),
        out_shape=jax.ShapeDtypeStruct((pairs,) + piece, down.dtype),
        in_specs=[SMEM] * 3 + [ANY] * 2,
        out_specs=VMEM,
        scratch_shapes=[pltpu.SemaphoreType.DMA((pairs, blocks, 2))],
        compiler_params=BIG,
    )(here, all_ids, slots, down, up)
    return here, all_ids, packed


def merge_factors(here, all_ids, slots, down, up, packed):
    replicas = lax.axis_size("replica")
    pairs, blocks = packed.shape[:2]
    paired = lax.ppermute(packed, "replica", [(i, i ^ 1) for i in range(replicas)])
    merged = pl.pallas_call(
        functools.partial(merge_kernel, replicas, blocks),
        out_shape=jax.ShapeDtypeStruct((pairs - 1,) + packed.shape[1:], down.dtype),
        in_specs=[SMEM] * 3 + [ANY] * 3,
        out_specs=VMEM,
        scratch_shapes=[pltpu.SemaphoreType.DMA((pairs - 1, blocks, 2))],
        compiler_params=BIG,
    )(here, all_ids, slots, down, up, paired)
    return paired, merged


def fetch_factors(merged):
    replicas = lax.axis_size("replica")
    return [
        lax.ppermute(
            merged[k - 1], "replica", [(i, (i + 2 * k) % replicas) for i in range(replicas)]
        )
        for k in range(1, replicas // 2)
    ]


def pick_factors(here, all_ids, slots, order, down, up, paired, fetched):
    replicas = lax.axis_size("replica")
    blocks = all_ids.shape[1]
    return pl.pallas_call(
        functools.partial(pick_kernel, replicas, blocks),
        out_shape=jax.ShapeDtypeStruct(paired.shape[1:], down.dtype),
        in_specs=[SMEM] * 4 + [ANY] * (3 + len(fetched)),
        out_specs=VMEM,
        scratch_shapes=[pltpu.SemaphoreType.DMA((blocks, 2))],
        compiler_params=BIG,
    )(here, all_ids, slots, order, down, up, paired, *fetched)


def sum_over_tensor(partial):
    size = lax.axis_size("tensor")
    if size != LINE:
        return lax.psum(partial, "tensor")
    for bit in (1, 2):
        partial = partial + lax.ppermute(
            partial, "tensor", [(i, i ^ bit) for i in range(size)]
        )
    return partial


def finish_kernel(order_ref, live_ref, end_ref, near_ref, far_ref, *refs):
    lasts = refs[:PARTS]
    sent_ref = refs[PARTS]
    passed_lasts = refs[PARTS + 1 : 2 * PARTS + 1]
    reduced_ref, factors_ref, result_ref = refs[2 * PARTS + 1 :]
    blocks = reduced_ref.shape[0]
    rows = near_ref.shape[0] // blocks
    depth = factors_ref.shape[2] - near_ref.shape[1]
    at_end = end_ref[0] == 1
    for i in range(blocks):
        b = order_ref[i]
        delta = lax.dot_general(
            reduced_ref[i],
            factors_ref[i, :, depth:],
            (((0,), (0,)), ((), ())),
            preferred_element_type=jnp.float32,
        )
        if i < 3:
            other = far_ref[pl.ds(i * rows, rows), :]
        else:
            other = jnp.concatenate([ref[...] for ref in lasts])
        if i > 0:
            if i < 3:
                passed = sent_ref[pl.ds((i - 1) * rows, rows), :]
            else:
                passed = jnp.concatenate([ref[...] for ref in passed_lasts])
            other = jnp.where(at_end, passed.astype(jnp.float32), other)
        total = near_ref[pl.ds(i * rows, rows), :] + other + 2.0 * delta
        live = lax.broadcasted_iota(jnp.int32, total.shape, 0) < live_ref[b]
        result_ref[pl.ds(pl.multiple_of(b * rows, rows), rows), :] = jnp.where(
            live, total, 0.0
        ).astype(result_ref.dtype)


def dot(a, b):
    return jnp.dot(a, b, preferred_element_type=jnp.float32)


def tie(*arrays):
    return lax.optimization_barrier(arrays)


def line_body(
    queries,
    keys,
    values,
    lengths,
    weight,
    down,
    up,
    ids,
    live_rows,
    slots,
):
    rows, width = queries.shape
    half = width // 2
    me = lax.axis_index("tensor")
    side = me // 2
    is_end = (me == 0) | (me == LINE - 1)
    near_at, far_at = side * half, (1 - side) * half
    ends = [(0, 1), (1, 0), (2, 3), (3, 2)]
    middle = [(1, 2), (2, 1)]
    outward = [(1, 0), (2, 3)]
    inward = [(0, 1), (3, 2)]
    order = jnp.array([[0, 1, 2, 3], [1, 0, 2, 3], [2, 3, 1, 0], [3, 2, 1, 0]], jnp.int32)[me]

    planes = lax.axis_size("groups") * lax.axis_size("replica")
    share = half // planes
    mine = lax.axis_index("groups") * lax.axis_size("replica") + lax.axis_index("replica")
    piece = lax.dynamic_slice_in_dim(weight, far_at + mine * share, share, 0)
    piece = lax.ppermute(piece, "tensor", inward)
    here, all_ids, packed = pair_factors(down, up, ids, slots)

    cut = rows // PARTS
    attended = attention(queries, keys, values, lengths)
    attended, packed = tie(attended, packed)
    piece, _ = tie(piece, attended)
    end_weight = lax.all_gather(piece, ("groups", "replica"), axis=0, tiled=True)
    near = lax.dynamic_slice_in_dim(attended, near_at, half, 1)
    far = lax.dynamic_slice_in_dim(attended, far_at, half, 1)
    nears = [near[p * cut : (p + 1) * cut] for p in range(PARTS)]
    fars = [far[p * cut : (p + 1) * cut] for p in range(PARTS)]
    e1, e2, e3, m1, m2, m3, m4 = ([] for _ in range(7))
    for p in range(PARTS):
        outer, inner = tie(jnp.where(is_end, fars[p], nears[p]), fars[p])
        e1.append(lax.ppermute(outer, "tensor", ends))
        m1.append(lax.ppermute(inner, "tensor", middle))
    paired, merged = merge_factors(here, all_ids, slots, down, up, packed)
    m1[0], merged = tie(m1[0], merged)
    fetched = fetch_factors(merged)
    for p in range(PARTS):
        outer, inner = tie(jnp.where(is_end, nears[p], m1[p]), e1[p])
        e2.append(lax.ppermute(outer, "tensor", ends))
        m2.append(lax.ppermute(inner, "tensor", middle))
    for p in range(PARTS):
        outer, inner = tie(m2[p], nears[p])
        e3.append(lax.ppermute(outer, "tensor", outward))
        m3.append(lax.ppermute(inner, "tensor", middle))
    for p in range(PARTS):
        m4.append(lax.ppermute(e2[p], "tensor", middle))
    far, _ = tie(far, e1[-1])

    near_rows = jnp.concatenate(
        nears
        + [jnp.where(is_end, e1[p], e2[p]) for p in range(PARTS)]
        + [jnp.where(is_end, e2[p], m1[p]) for p in range(PARTS)]
        + [jnp.where(is_end, e3[p], m2[p]) for p in range(PARTS)]
    )
    near_weight = lax.dynamic_slice_in_dim(weight, near_at, half, 0)
    far_weight = lax.dynamic_slice_in_dim(weight, far_at, half, 0)
    far_rows = jnp.concatenate([far] + e1 + m3)

    factors = pick_factors(here, all_ids, slots, order, down, up, paired, fetched)
    depth = down.shape[2]
    blocks = ids.shape[0]
    columns = lax.dynamic_slice_in_dim(near_rows, (me % 2) * depth, depth, 1)
    partial_rank = jnp.einsum(
        "bri,bki->bkr",
        columns.reshape(blocks, rows, depth),
        factors[:, :, :depth],
        preferred_element_type=jnp.float32,
    )
    back = jnp.array([[0, 1, 2, 3], [1, 0, 2, 3], [3, 2, 0, 1], [3, 2, 1, 0]], jnp.int32)[me]
    reduced = sum_over_tensor(partial_rank[back])[order].astype(jnp.bfloat16)

    near_out = dot(near_rows, near_weight)
    far_out = dot(far_rows, far_weight)
    sent = dot(jnp.concatenate([far] + m3), end_weight).astype(jnp.bfloat16)
    sent, near_out, far_out, reduced, *m4 = tie(sent, near_out, far_out, reduced, *m4)
    sent = lax.ppermute(sent, "tensor", outward)
    passed = [
        lax.ppermute(dot(rows, end_weight).astype(jnp.bfloat16), "tensor", outward) for rows in m4
    ]
    last_out = [dot(rows, far_weight) for rows in m4]
    return pl.pallas_call(
        finish_kernel,
        out_shape=jax.ShapeDtypeStruct(near_out.shape, jnp.bfloat16),
        in_specs=[SMEM] * 3 + [VMEM] * (5 + 2 * PARTS),
        out_specs=VMEM,
        compiler_params=BIG,
    )(
        order,
        live_rows,
        is_end.astype(jnp.int32)[None],
        near_out,
        far_out,
        *last_out,
        sent,
        *passed,
        reduced,
        factors,
    )


def body(
    queries,
    keys,
    values,
    lengths,
    output_projection_weight,
    adapter_down_factors,
    adapter_up_factors,
    block_adapter_index,
    block_live_rows,
    adapter_storage_slot,
):
    rows = queries.shape[0]
    replica_rows = rows * lax.axis_size("tensor")
    blocks = block_adapter_index.shape[0]
    block_rows = replica_rows // blocks
    down = jnp.swapaxes(adapter_down_factors, 1, 2)
    up = adapter_up_factors
    if lax.axis_size("tensor") == LINE and block_rows == rows:
        return line_body(
            queries,
            keys,
            values,
            lengths,
            output_projection_weight,
            down,
            up,
            block_adapter_index,
            block_live_rows,
            adapter_storage_slot,
        )
    here, all_ids, packed = pair_factors(down, up, block_adapter_index, adapter_storage_slot)
    paired, merged = merge_factors(here, all_ids, adapter_storage_slot, down, up, packed)
    fetched = fetch_factors(merged)
    attended = lax.all_gather(
        attention(queries, keys, values, lengths), "tensor", axis=0, tiled=True
    )
    order = jnp.arange(blocks, dtype=jnp.int32)
    factors = pick_factors(
        here, all_ids, adapter_storage_slot, order, down, up, paired, fetched
    )
    depth = down.shape[2]
    columns = lax.dynamic_slice_in_dim(
        attended, lax.axis_index("tensor") * depth, depth, 1
    ).reshape(blocks, block_rows, depth)
    partial_rank = jnp.einsum(
        "bri,bki->bkr", columns, factors[:, :, :depth], preferred_element_type=jnp.float32
    )
    reduced = sum_over_tensor(partial_rank).astype(jnp.bfloat16)
    base = dot(attended, output_projection_weight)
    delta = jnp.einsum(
        "bkr,bkc->brc", reduced, factors[:, :, depth:], preferred_element_type=jnp.float32
    )
    live = (jnp.arange(block_rows)[None, :] < block_live_rows[:, None])[..., None]
    base = base.reshape(delta.shape)
    return (
        jnp.where(live, base + 2.0 * delta, 0.0)
        .astype(jnp.bfloat16)
        .reshape(replica_rows, base.shape[2])
    )


def solution(mesh):
    placed = (
        P(("groups", "replica", "tensor"), None),
        P(("groups", "replica", "tensor"), None, None),
        P(("groups", "replica", "tensor"), None, None),
        P(("groups", "replica", "tensor")),
        P(None, "tensor"),
        P(("groups", "replica"), "tensor", None),
        P(("groups", "replica"), None, "tensor"),
        P(("groups", "replica")),
        P(("groups", "replica")),
        P("groups"),
    )
    return jax.shard_map(
        body,
        mesh=mesh,
        in_specs=placed,
        out_specs=P(("groups", "replica"), "tensor"),
        check_vma=False,
    )
```

```python
import functools

import jax
import jax.numpy as jnp
from jax import lax
from jax.experimental import pallas as pl
from jax.experimental.pallas import tpu as pltpu
from jax.sharding import PartitionSpec as P

QUERY_HEAD_COUNT = 64
KVH = 8
HEAD_SIZE = 128
LINE = 4
PARTS = 2
ANY = pl.BlockSpec(memory_space=pl.ANY)
SMEM = pl.BlockSpec(memory_space=pltpu.SMEM)
VMEM = pl.BlockSpec(memory_space=pltpu.VMEM)
BIG = pltpu.CompilerParams(vmem_limit_bytes=40 * 2**20)


def attention(queries, keys, values, lengths):
    row_count = queries.shape[0]
    span = keys.shape[1]
    group_size = QUERY_HEAD_COUNT // KVH
    query_heads = queries.reshape(row_count, KVH, group_size, HEAD_SIZE)
    key_heads = keys.reshape(row_count, span, KVH, HEAD_SIZE)
    value_heads = values.reshape(row_count, span, KVH, HEAD_SIZE).astype(jnp.float32)
    scores = jnp.einsum(
        "rkgd,rpkd->rkgp", query_heads, key_heads, preferred_element_type=jnp.float32
    ) * HEAD_SIZE ** (-0.5)
    visible = (jnp.arange(span)[None, :] < lengths[:, None])[:, None, None, :]
    scores = jnp.where(visible, scores, -1e30)
    highest = jnp.max(scores, axis=3, keepdims=True)
    weights = jnp.where(visible, jnp.exp(scores - highest), 0.0)
    totals = jnp.sum(weights, axis=3)
    summed = jnp.einsum("rkgp,rpkd->rkgd", weights, value_heads)
    return (
        (summed / totals[..., None])
        .reshape(row_count, QUERY_HEAD_COUNT * HEAD_SIZE)
        .astype(jnp.bfloat16)
    )


def slot_of(replicas, ids_ref, slots_ref, here, target, b):
    return slots_ref[ids_ref[lax.rem(target - here + replicas, replicas), b]]


def factor_copies(act, at, down_ref, up_ref, target, sems):
    depth = down_ref.shape[2]
    act(pltpu.make_async_copy(down_ref.at[at], target.at[:, pl.ds(0, depth)], sems.at[0]))
    act(pltpu.make_async_copy(up_ref.at[at], target.at[:, pl.ds(depth, up_ref.shape[2])], sems.at[1]))


def pair_kernel(replicas, blocks, here_ref, ids_ref, slots_ref, down_ref, up_ref, out_ref, sems):
    own = down_ref.shape[0]
    pairs = replicas // 2
    here = here_ref[0]
    pair, core = lax.div(here, 2), lax.rem(here, 2)

    def each(act):
        for k in range(pairs):
            target = lax.rem(pair + k, pairs) * 2 + 1 - core
            for b in range(blocks):
                slot = slot_of(replicas, ids_ref, slots_ref, here, target, b)

                @pl.when(lax.div(slot, own) == here)
                def _():
                    factor_copies(
                        act, lax.rem(slot, own), down_ref, up_ref, out_ref.at[k, b], sems.at[k, b]
                    )

    each(lambda copy: copy.start())
    each(lambda copy: copy.wait())


def merge_kernel(
    replicas, blocks, here_ref, ids_ref, slots_ref, down_ref, up_ref, paired_ref, out_ref, sems
):
    own = down_ref.shape[0]
    pairs = replicas // 2
    here = here_ref[0]
    pair, core = lax.div(here, 2), lax.rem(here, 2)

    def each(act):
        for k in range(1, pairs):
            to = lax.rem(pair + k, pairs)
            target = to * 2 + core
            for b in range(blocks):
                slot = slot_of(replicas, ids_ref, slots_ref, here, target, b)
                home = lax.div(slot, own)
                place = out_ref.at[to, b]

                @pl.when(home == here)
                def _():
                    factor_copies(
                        act, lax.rem(slot, own), down_ref, up_ref, place, sems.at[k - 1, b]
                    )

                @pl.when(home == pair * 2 + 1 - core)
                def _():
                    act(pltpu.make_async_copy(paired_ref.at[k, b], place, sems.at[k - 1, b, 0]))

    each(lambda copy: copy.start())
    each(lambda copy: copy.wait())


def pick_kernel(
    replicas,
    blocks,
    here_ref,
    ids_ref,
    slots_ref,
    order_ref,
    down_ref,
    up_ref,
    paired_ref,
    fetched_ref,
    out_ref,
    sems,
):
    own = down_ref.shape[0]
    pairs = replicas // 2
    here = here_ref[0]
    pair = lax.div(here, 2)

    def each(act):
        for i in range(blocks):
            b = order_ref[i]
            slot = slots_ref[ids_ref[0, b]]
            home = lax.div(slot, own)
            shift = lax.rem(pair - lax.div(home, 2) + pairs, pairs)

            @pl.when(home == here)
            def _():
                factor_copies(act, lax.rem(slot, own), down_ref, up_ref, out_ref.at[i], sems.at[i])

            @pl.when((shift == 0) & (home != here))
            def _():
                act(pltpu.make_async_copy(paired_ref.at[0, b], out_ref.at[i], sems.at[i, 0]))

            @pl.when(shift != 0)
            def _():
                act(
                    pltpu.make_async_copy(
                        fetched_ref.at[lax.div(home, 2), b], out_ref.at[i], sems.at[i, 0]
                    )
                )

    each(lambda copy: copy.start())
    each(lambda copy: copy.wait())


def pair_factors(down, up, ids, slots):
    replicas = lax.axis_size("replica")
    here = lax.axis_index("replica").astype(jnp.int32)[None]
    blocks = ids.shape[0]
    all_ids = jnp.stack(
        [ids]
        + [
            lax.ppermute(ids, "replica", [(i, (i - shift) % replicas) for i in range(replicas)])
            for shift in range(1, replicas)
        ]
    )
    pairs = replicas // 2
    piece = (blocks, down.shape[1], down.shape[2] + up.shape[2])
    packed = pl.pallas_call(
        functools.partial(pair_kernel, replicas, blocks),
        out_shape=jax.ShapeDtypeStruct((pairs,) + piece, down.dtype),
        in_specs=[SMEM] * 3 + [ANY] * 2,
        out_specs=VMEM,
        scratch_shapes=[pltpu.SemaphoreType.DMA((pairs, blocks, 2))],
        compiler_params=BIG,
    )(here, all_ids, slots, down, up)
    return here, all_ids, packed


def merge_factors(here, all_ids, slots, down, up, packed):
    replicas = lax.axis_size("replica")
    pairs, blocks = packed.shape[:2]
    paired = lax.ppermute(packed, "replica", [(i, i ^ 1) for i in range(replicas)])
    merged = pl.pallas_call(
        functools.partial(merge_kernel, replicas, blocks),
        out_shape=jax.ShapeDtypeStruct(packed.shape, down.dtype),
        in_specs=[SMEM] * 3 + [ANY] * 3,
        out_specs=VMEM,
        scratch_shapes=[pltpu.SemaphoreType.DMA((pairs - 1, blocks, 2))],
        compiler_params=BIG,
    )(here, all_ids, slots, down, up, paired)
    return paired, merged


def fetch_factors(merged):
    replicas = lax.axis_size("replica")
    groups = [list(range(core, replicas, 2)) for core in range(2)]
    return lax.all_to_all(
        merged, "replica", split_axis=0, concat_axis=0, tiled=True, axis_index_groups=groups
    )


def pick_factors(here, all_ids, slots, order, down, up, paired, fetched):
    replicas = lax.axis_size("replica")
    blocks = all_ids.shape[1]
    return pl.pallas_call(
        functools.partial(pick_kernel, replicas, blocks),
        out_shape=jax.ShapeDtypeStruct(paired.shape[1:], down.dtype),
        in_specs=[SMEM] * 4 + [ANY] * 4,
        out_specs=VMEM,
        scratch_shapes=[pltpu.SemaphoreType.DMA((blocks, 2))],
        compiler_params=BIG,
    )(here, all_ids, slots, order, down, up, paired, fetched)


def sum_over_tensor(partial):
    size = lax.axis_size("tensor")
    if size != LINE:
        return lax.psum(partial, "tensor")
    for bit in (1, 2):
        partial = partial + lax.ppermute(
            partial, "tensor", [(i, i ^ bit) for i in range(size)]
        )
    return partial


def finish_kernel(order_ref, live_ref, end_ref, near_ref, early_ref, late_ref, *refs):
    passed_refs = refs[:3]
    reduced_ref, factors_ref, result_ref = refs[3:]
    blocks = reduced_ref.shape[0]
    rows = near_ref.shape[0] // blocks
    depth = factors_ref.shape[2] - near_ref.shape[1]
    at_end = end_ref[0] == 1
    for i in range(blocks):
        b = order_ref[i]
        delta = lax.dot_general(
            reduced_ref[i],
            factors_ref[i, :, depth:],
            (((0,), (0,)), ((), ())),
            preferred_element_type=jnp.float32,
        )
        other_ref = early_ref if i < 2 else late_ref
        other = other_ref[pl.ds(i % 2 * rows, rows), :]
        if i > 0:
            other = jnp.where(at_end, passed_refs[i - 1][...].astype(jnp.float32), other)
        total = near_ref[pl.ds(i * rows, rows), :] + other + 2.0 * delta
        live = lax.broadcasted_iota(jnp.int32, total.shape, 0) < live_ref[b]
        result_ref[pl.ds(pl.multiple_of(b * rows, rows), rows), :] = jnp.where(
            live, total, 0.0
        ).astype(result_ref.dtype)


def dot(a, b):
    return jnp.dot(a, b, preferred_element_type=jnp.float32)


def tie(*arrays):
    return lax.optimization_barrier(arrays)


def line_body(
    queries,
    keys,
    values,
    lengths,
    weight,
    down,
    up,
    ids,
    live_rows,
    slots,
):
    rows, width = queries.shape
    half = width // 2
    me = lax.axis_index("tensor")
    side = me // 2
    is_end = (me == 0) | (me == LINE - 1)
    near_at, far_at = side * half, (1 - side) * half
    ends = [(0, 1), (1, 0), (2, 3), (3, 2)]
    middle = [(1, 2), (2, 1)]
    outward = [(1, 0), (2, 3)]
    inward = [(0, 1), (3, 2)]
    order = jnp.array([[0, 1, 2, 3], [1, 0, 2, 3], [2, 3, 1, 0], [3, 2, 1, 0]], jnp.int32)[me]

    planes = lax.axis_size("groups") * lax.axis_size("replica")
    share = half // planes
    mine = lax.axis_index("groups") * lax.axis_size("replica") + lax.axis_index("replica")
    piece = lax.dynamic_slice_in_dim(weight, far_at + mine * share, share, 0)
    piece = lax.ppermute(piece, "tensor", inward)
    here, all_ids, packed = pair_factors(down, up, ids, slots)

    cut = rows // PARTS
    attended = attention(queries, keys, values, lengths)
    attended, packed = tie(attended, packed)
    piece, _ = tie(piece, attended)
    end_weight = lax.all_gather(piece, ("groups", "replica"), axis=0, tiled=True)
    near = lax.dynamic_slice_in_dim(attended, near_at, half, 1)
    far = lax.dynamic_slice_in_dim(attended, far_at, half, 1)
    nears = [near[p * cut : (p + 1) * cut] for p in range(PARTS)]
    fars = [far[p * cut : (p + 1) * cut] for p in range(PARTS)]
    e1, e2, m1, m2 = ([] for _ in range(4))
    for p in range(PARTS):
        outer, inner = tie(jnp.where(is_end, fars[p], nears[p]), fars[p])
        e1.append(lax.ppermute(outer, "tensor", ends))
        m1.append(lax.ppermute(inner, "tensor", middle))
    paired, merged = merge_factors(here, all_ids, slots, down, up, packed)
    m1[0], merged = tie(m1[0], merged)
    fetched = fetch_factors(merged)
    for p in range(PARTS):
        outer, inner = tie(jnp.where(is_end, nears[p], m1[p]), e1[p])
        e2.append(lax.ppermute(outer, "tensor", ends))
        m2.append(lax.ppermute(inner, "tensor", middle))
    far_half = lax.dynamic_slice_in_dim(weight, far_at, half, 0)
    far, _ = tie(far, e1[-1])
    early_out = dot(jnp.concatenate([far] + e1), far_half)
    e2[-1], early_out = tie(e2[-1], early_out)
    m3, m4, e3 = [], [], []
    for p in range(PARTS):
        inner, *_ = tie(nears[p], *m2)
        e3.append(lax.ppermute(m2[p], "tensor", outward))
        m3.append(lax.ppermute(inner, "tensor", middle))
        m4.append(lax.ppermute(e2[p], "tensor", middle))

    near_rows = jnp.concatenate(
        nears
        + [jnp.where(is_end, e1[p], e2[p]) for p in range(PARTS)]
        + [jnp.where(is_end, e2[p], m1[p]) for p in range(PARTS)]
        + [jnp.where(is_end, e3[p], m2[p]) for p in range(PARTS)]
    )
    near_weight = lax.dynamic_slice_in_dim(weight, near_at, half, 0)

    pick_order, *_ = tie(order, *e3)
    factors = pick_factors(here, all_ids, slots, pick_order, down, up, paired, fetched)
    depth = down.shape[2]
    blocks = ids.shape[0]
    columns = lax.dynamic_slice_in_dim(near_rows, (me % 2) * depth, depth, 1)
    partial_rank = jnp.einsum(
        "bri,bki->bkr",
        columns.reshape(blocks, rows, depth),
        factors[:, :, :depth],
        preferred_element_type=jnp.float32,
    )
    back = jnp.array([[0, 1, 2, 3], [1, 0, 2, 3], [3, 2, 0, 1], [3, 2, 1, 0]], jnp.int32)[me]
    reduced = sum_over_tensor(partial_rank[back])[order].astype(jnp.bfloat16)

    near_out = dot(near_rows, near_weight)
    near_out, _ = tie(near_out, partial_rank)
    inner = jnp.concatenate(m3)
    inner_sent = dot(jnp.concatenate([far, inner]), end_weight).astype(jnp.bfloat16)
    inner_passed = lax.ppermute(inner_sent, "tensor", outward)
    inner_sent, near_out, reduced, *m4 = tie(inner_sent, near_out, reduced, *m4)
    last = jnp.concatenate(m4)
    last_sent = dot(last, end_weight).astype(jnp.bfloat16)
    last_passed = lax.ppermute(last_sent, "tensor", outward)
    inner, _ = tie(inner, last_sent)
    late_out = dot(jnp.concatenate([inner, last]), far_half)
    return pl.pallas_call(
        finish_kernel,
        out_shape=jax.ShapeDtypeStruct(near_out.shape, jnp.bfloat16),
        in_specs=[SMEM] * 3 + [VMEM] * 8,
        out_specs=VMEM,
        compiler_params=BIG,
    )(
        order,
        live_rows,
        is_end.astype(jnp.int32)[None],
        near_out,
        early_out,
        late_out,
        inner_passed[:rows],
        inner_passed[rows:],
        last_passed,
        reduced,
        factors,
    )


def body(
    queries,
    keys,
    values,
    lengths,
    output_projection_weight,
    adapter_down_factors,
    adapter_up_factors,
    block_adapter_index,
    block_live_rows,
    adapter_storage_slot,
):
    rows = queries.shape[0]
    replica_rows = rows * lax.axis_size("tensor")
    blocks = block_adapter_index.shape[0]
    block_rows = replica_rows // blocks
    down = jnp.swapaxes(adapter_down_factors, 1, 2)
    up = adapter_up_factors
    if lax.axis_size("tensor") == LINE and block_rows == rows:
        return line_body(
            queries,
            keys,
            values,
            lengths,
            output_projection_weight,
            down,
            up,
            block_adapter_index,
            block_live_rows,
            adapter_storage_slot,
        )
    here, all_ids, packed = pair_factors(down, up, block_adapter_index, adapter_storage_slot)
    paired, merged = merge_factors(here, all_ids, adapter_storage_slot, down, up, packed)
    fetched = fetch_factors(merged)
    attended = lax.all_gather(
        attention(queries, keys, values, lengths), "tensor", axis=0, tiled=True
    )
    order = jnp.arange(blocks, dtype=jnp.int32)
    factors = pick_factors(
        here, all_ids, adapter_storage_slot, order, down, up, paired, fetched
    )
    depth = down.shape[2]
    columns = lax.dynamic_slice_in_dim(
        attended, lax.axis_index("tensor") * depth, depth, 1
    ).reshape(blocks, block_rows, depth)
    partial_rank = jnp.einsum(
        "bri,bki->bkr", columns, factors[:, :, :depth], preferred_element_type=jnp.float32
    )
    reduced = sum_over_tensor(partial_rank).astype(jnp.bfloat16)
    base = dot(attended, output_projection_weight)
    delta = jnp.einsum(
        "bkr,bkc->brc", reduced, factors[:, :, depth:], preferred_element_type=jnp.float32
    )
    live = (jnp.arange(block_rows)[None, :] < block_live_rows[:, None])[..., None]
    base = base.reshape(delta.shape)
    return (
        jnp.where(live, base + 2.0 * delta, 0.0)
        .astype(jnp.bfloat16)
        .reshape(replica_rows, base.shape[2])
    )


def solution(mesh):
    placed = (
        P(("groups", "replica", "tensor"), None),
        P(("groups", "replica", "tensor"), None, None),
        P(("groups", "replica", "tensor"), None, None),
        P(("groups", "replica", "tensor")),
        P(None, "tensor"),
        P(("groups", "replica"), "tensor", None),
        P(("groups", "replica"), None, "tensor"),
        P(("groups", "replica")),
        P(("groups", "replica")),
        P("groups"),
    )
    return jax.shard_map(
        body,
        mesh=mesh,
        in_specs=placed,
        out_specs=P(("groups", "replica"), "tensor"),
        check_vma=False,
    )
```

```python
import functools

import jax
import jax.numpy as jnp
from jax import lax
from jax.experimental import pallas as pl
from jax.experimental.pallas import tpu as pltpu
from jax.sharding import PartitionSpec as P

QUERY_HEAD_COUNT = 64
KVH = 8
HEAD_SIZE = 128
LINE = 4
PARTS = 2
ANY = pl.BlockSpec(memory_space=pl.ANY)
SMEM = pl.BlockSpec(memory_space=pltpu.SMEM)
VMEM = pl.BlockSpec(memory_space=pltpu.VMEM)
BIG = pltpu.CompilerParams(vmem_limit_bytes=40 * 2**20)


def attention(queries, keys, values, lengths):
    row_count = queries.shape[0]
    span = keys.shape[1]
    group_size = QUERY_HEAD_COUNT // KVH
    query_heads = queries.reshape(row_count, KVH, group_size, HEAD_SIZE)
    key_heads = keys.reshape(row_count, span, KVH, HEAD_SIZE)
    value_heads = values.reshape(row_count, span, KVH, HEAD_SIZE).astype(jnp.float32)
    scores = jnp.einsum(
        "rkgd,rpkd->rkgp", query_heads, key_heads, preferred_element_type=jnp.float32
    ) * HEAD_SIZE ** (-0.5)
    visible = (jnp.arange(span)[None, :] < lengths[:, None])[:, None, None, :]
    scores = jnp.where(visible, scores, -1e30)
    highest = jnp.max(scores, axis=3, keepdims=True)
    weights = jnp.where(visible, jnp.exp(scores - highest), 0.0)
    totals = jnp.sum(weights, axis=3)
    summed = jnp.einsum("rkgp,rpkd->rkgd", weights, value_heads)
    return (
        (summed / totals[..., None])
        .reshape(row_count, QUERY_HEAD_COUNT * HEAD_SIZE)
        .astype(jnp.bfloat16)
    )


def slot_of(replicas, ids_ref, slots_ref, here, target, b):
    return slots_ref[ids_ref[lax.rem(target - here + replicas, replicas), b]]


def factor_copies(act, at, down_ref, up_ref, target, sems):
    depth = down_ref.shape[2]
    act(pltpu.make_async_copy(down_ref.at[at], target.at[:, pl.ds(0, depth)], sems.at[0]))
    act(pltpu.make_async_copy(up_ref.at[at], target.at[:, pl.ds(depth, up_ref.shape[2])], sems.at[1]))


def pair_kernel(replicas, blocks, here_ref, ids_ref, slots_ref, down_ref, up_ref, out_ref, sems):
    own = down_ref.shape[0]
    pairs = replicas // 2
    here = here_ref[0]
    pair, core = lax.div(here, 2), lax.rem(here, 2)

    def each(act):
        for k in range(pairs):
            target = lax.rem(pair + k, pairs) * 2 + 1 - core
            for b in range(blocks):
                slot = slot_of(replicas, ids_ref, slots_ref, here, target, b)

                @pl.when(lax.div(slot, own) == here)
                def _():
                    factor_copies(
                        act, lax.rem(slot, own), down_ref, up_ref, out_ref.at[k, b], sems.at[k, b]
                    )

    each(lambda copy: copy.start())
    each(lambda copy: copy.wait())


def merge_kernel(
    replicas, blocks, here_ref, ids_ref, slots_ref, down_ref, up_ref, paired_ref, out_ref, sems
):
    own = down_ref.shape[0]
    pairs = replicas // 2
    here = here_ref[0]
    pair, core = lax.div(here, 2), lax.rem(here, 2)

    def each(act):
        for k in range(1, pairs):
            to = lax.rem(pair + k, pairs)
            target = to * 2 + core
            for b in range(blocks):
                slot = slot_of(replicas, ids_ref, slots_ref, here, target, b)
                home = lax.div(slot, own)
                place = out_ref.at[to, b]

                @pl.when(home == here)
                def _():
                    factor_copies(
                        act, lax.rem(slot, own), down_ref, up_ref, place, sems.at[k - 1, b]
                    )

                @pl.when(home == pair * 2 + 1 - core)
                def _():
                    act(pltpu.make_async_copy(paired_ref.at[k, b], place, sems.at[k - 1, b, 0]))

    each(lambda copy: copy.start())
    each(lambda copy: copy.wait())


def pick_kernel(
    replicas,
    blocks,
    here_ref,
    ids_ref,
    slots_ref,
    order_ref,
    down_ref,
    up_ref,
    paired_ref,
    fetched_ref,
    out_ref,
    sems,
):
    own = down_ref.shape[0]
    pairs = replicas // 2
    here = here_ref[0]
    pair = lax.div(here, 2)

    def each(act):
        for i in range(blocks):
            b = order_ref[i]
            slot = slots_ref[ids_ref[0, b]]
            home = lax.div(slot, own)
            shift = lax.rem(pair - lax.div(home, 2) + pairs, pairs)

            @pl.when(home == here)
            def _():
                factor_copies(act, lax.rem(slot, own), down_ref, up_ref, out_ref.at[i], sems.at[i])

            @pl.when((shift == 0) & (home != here))
            def _():
                act(pltpu.make_async_copy(paired_ref.at[0, b], out_ref.at[i], sems.at[i, 0]))

            @pl.when(shift != 0)
            def _():
                act(
                    pltpu.make_async_copy(
                        fetched_ref.at[lax.div(home, 2), b], out_ref.at[i], sems.at[i, 0]
                    )
                )

    each(lambda copy: copy.start())
    each(lambda copy: copy.wait())


def pair_factors(down, up, ids, slots):
    replicas = lax.axis_size("replica")
    here = lax.axis_index("replica").astype(jnp.int32)[None]
    blocks = ids.shape[0]
    all_ids = jnp.stack(
        [ids]
        + [
            lax.ppermute(ids, "replica", [(i, (i - shift) % replicas) for i in range(replicas)])
            for shift in range(1, replicas)
        ]
    )
    pairs = replicas // 2
    piece = (blocks, down.shape[1], down.shape[2] + up.shape[2])
    packed = pl.pallas_call(
        functools.partial(pair_kernel, replicas, blocks),
        out_shape=jax.ShapeDtypeStruct((pairs,) + piece, down.dtype),
        in_specs=[SMEM] * 3 + [ANY] * 2,
        out_specs=VMEM,
        scratch_shapes=[pltpu.SemaphoreType.DMA((pairs, blocks, 2))],
        compiler_params=BIG,
    )(here, all_ids, slots, down, up)
    return here, all_ids, packed


def merge_factors(here, all_ids, slots, down, up, packed):
    replicas = lax.axis_size("replica")
    pairs, blocks = packed.shape[:2]
    paired = lax.ppermute(packed, "replica", [(i, i ^ 1) for i in range(replicas)])
    merged = pl.pallas_call(
        functools.partial(merge_kernel, replicas, blocks),
        out_shape=jax.ShapeDtypeStruct(packed.shape, down.dtype),
        in_specs=[SMEM] * 3 + [ANY] * 3,
        out_specs=VMEM,
        scratch_shapes=[pltpu.SemaphoreType.DMA((pairs - 1, blocks, 2))],
        compiler_params=BIG,
    )(here, all_ids, slots, down, up, paired)
    return paired, merged


def fetch_factors(merged):
    replicas = lax.axis_size("replica")
    groups = [list(range(core, replicas, 2)) for core in range(2)]
    return lax.all_to_all(
        merged, "replica", split_axis=0, concat_axis=0, tiled=True, axis_index_groups=groups
    )


def pick_factors(here, all_ids, slots, order, down, up, paired, fetched):
    replicas = lax.axis_size("replica")
    blocks = all_ids.shape[1]
    return pl.pallas_call(
        functools.partial(pick_kernel, replicas, blocks),
        out_shape=jax.ShapeDtypeStruct(paired.shape[1:], down.dtype),
        in_specs=[SMEM] * 4 + [ANY] * 4,
        out_specs=VMEM,
        scratch_shapes=[pltpu.SemaphoreType.DMA((blocks, 2))],
        compiler_params=BIG,
    )(here, all_ids, slots, order, down, up, paired, fetched)


def sum_over_tensor(partial):
    size = lax.axis_size("tensor")
    if size != LINE:
        return lax.psum(partial, "tensor")
    for bit in (1, 2):
        partial = partial + lax.ppermute(
            partial, "tensor", [(i, i ^ bit) for i in range(size)]
        )
    return partial


def finish_kernel(order_ref, live_ref, end_ref, near_ref, early_ref, late_ref, *refs):
    passed_refs = refs[:3]
    reduced_ref, factors_ref, result_ref = refs[3:]
    blocks = reduced_ref.shape[0]
    rows = near_ref.shape[0] // blocks
    depth = factors_ref.shape[2] - near_ref.shape[1]
    at_end = end_ref[0] == 1
    for i in range(blocks):
        b = order_ref[i]
        delta = lax.dot_general(
            reduced_ref[i],
            factors_ref[i, :, depth:],
            (((0,), (0,)), ((), ())),
            preferred_element_type=jnp.float32,
        )
        other_ref = early_ref if i < 2 else late_ref
        other = other_ref[pl.ds(i % 2 * rows, rows), :]
        if i > 0:
            other = jnp.where(at_end, passed_refs[i - 1][...].astype(jnp.float32), other)
        total = near_ref[pl.ds(i * rows, rows), :] + other + 2.0 * delta
        live = lax.broadcasted_iota(jnp.int32, total.shape, 0) < live_ref[b]
        result_ref[pl.ds(pl.multiple_of(b * rows, rows), rows), :] = jnp.where(
            live, total, 0.0
        ).astype(result_ref.dtype)


def dot(a, b):
    return jnp.dot(a, b, preferred_element_type=jnp.float32)


def tie(*arrays):
    return lax.optimization_barrier(arrays)


def line_body(
    queries,
    keys,
    values,
    lengths,
    weight,
    down,
    up,
    ids,
    live_rows,
    slots,
):
    rows, width = queries.shape
    half = width // 2
    me = lax.axis_index("tensor")
    side = me // 2
    is_end = (me == 0) | (me == LINE - 1)
    near_at, far_at = side * half, (1 - side) * half
    ends = [(0, 1), (1, 0), (2, 3), (3, 2)]
    middle = [(1, 2), (2, 1)]
    outward = [(1, 0), (2, 3)]
    inward = [(0, 1), (3, 2)]
    order = jnp.array([[0, 1, 2, 3], [1, 0, 2, 3], [2, 3, 1, 0], [3, 2, 1, 0]], jnp.int32)[me]

    planes = lax.axis_size("groups") * lax.axis_size("replica")
    share = half // planes
    mine = lax.axis_index("groups") * lax.axis_size("replica") + lax.axis_index("replica")
    piece = lax.dynamic_slice_in_dim(weight, far_at + mine * share, share, 0)
    piece = lax.ppermute(piece, "tensor", inward)
    here, all_ids, packed = pair_factors(down, up, ids, slots)

    cut = rows // PARTS
    attended = attention(queries, keys, values, lengths)
    attended, packed = tie(attended, packed)
    piece, _ = tie(piece, attended)
    end_weight = lax.all_gather(piece, ("groups", "replica"), axis=0, tiled=True)
    near = lax.dynamic_slice_in_dim(attended, near_at, half, 1)
    far = lax.dynamic_slice_in_dim(attended, far_at, half, 1)
    nears = [near[p * cut : (p + 1) * cut] for p in range(PARTS)]
    fars = [far[p * cut : (p + 1) * cut] for p in range(PARTS)]
    e1, e2, m1, m2 = ([] for _ in range(4))
    for p in range(PARTS):
        outer, inner = tie(jnp.where(is_end, fars[p], nears[p]), fars[p])
        e1.append(lax.ppermute(outer, "tensor", ends))
        m1.append(lax.ppermute(inner, "tensor", middle))
    paired, merged = merge_factors(here, all_ids, slots, down, up, packed)
    m1[0], merged = tie(m1[0], merged)
    fetched = fetch_factors(merged)
    for p in range(PARTS):
        outer, inner = tie(jnp.where(is_end, nears[p], m1[p]), e1[p])
        e2.append(lax.ppermute(outer, "tensor", ends))
        m2.append(lax.ppermute(inner, "tensor", middle))
    far_half = lax.dynamic_slice_in_dim(weight, far_at, half, 0)
    far, _ = tie(far, e1[-1])
    early_out = dot(jnp.concatenate([far] + e1), far_half)
    e2[-1], early_out = tie(e2[-1], early_out)
    m3, m4, e3 = [], [], []
    for p in range(PARTS):
        inner, *_ = tie(nears[p], *m2, *e2[:1])
        e3.append(lax.ppermute(m2[p], "tensor", outward))
        m3.append(lax.ppermute(inner, "tensor", middle))
        m4.append(lax.ppermute(e2[p], "tensor", middle))

    near_rows = jnp.concatenate(
        nears
        + [jnp.where(is_end, e1[p], e2[p]) for p in range(PARTS)]
        + [jnp.where(is_end, e2[p], m1[p]) for p in range(PARTS)]
        + [jnp.where(is_end, e3[p], m2[p]) for p in range(PARTS)]
    )
    near_weight = lax.dynamic_slice_in_dim(weight, near_at, half, 0)

    pick_order, *_ = tie(order, *e3)
    factors = pick_factors(here, all_ids, slots, pick_order, down, up, paired, fetched)
    depth = down.shape[2]
    blocks = ids.shape[0]
    columns = lax.dynamic_slice_in_dim(near_rows, (me % 2) * depth, depth, 1)
    partial_rank = jnp.einsum(
        "bri,bki->bkr",
        columns.reshape(blocks, rows, depth),
        factors[:, :, :depth],
        preferred_element_type=jnp.float32,
    )
    back = jnp.array([[0, 1, 2, 3], [1, 0, 2, 3], [3, 2, 0, 1], [3, 2, 1, 0]], jnp.int32)[me]
    reduced = sum_over_tensor(partial_rank[back])[order].astype(jnp.bfloat16)

    near_out = dot(near_rows, near_weight)
    near_out, _ = tie(near_out, partial_rank)
    inner = jnp.concatenate(m3)
    inner_sent = dot(jnp.concatenate([far, inner]), end_weight).astype(jnp.bfloat16)
    inner_passed = lax.ppermute(inner_sent, "tensor", outward)
    inner_sent, *m4 = tie(inner_sent, *m4)
    last = jnp.concatenate(m4)
    last_sent = dot(last, end_weight).astype(jnp.bfloat16)
    last_passed = lax.ppermute(last_sent, "tensor", outward)
    inner, _ = tie(inner, last_sent)
    late_out = dot(jnp.concatenate([inner, last]), far_half)
    return pl.pallas_call(
        finish_kernel,
        out_shape=jax.ShapeDtypeStruct(near_out.shape, jnp.bfloat16),
        in_specs=[SMEM] * 3 + [VMEM] * 8,
        out_specs=VMEM,
        compiler_params=BIG,
    )(
        order,
        live_rows,
        is_end.astype(jnp.int32)[None],
        near_out,
        early_out,
        late_out,
        inner_passed[:rows],
        inner_passed[rows:],
        last_passed,
        reduced,
        factors,
    )


def body(
    queries,
    keys,
    values,
    lengths,
    output_projection_weight,
    adapter_down_factors,
    adapter_up_factors,
    block_adapter_index,
    block_live_rows,
    adapter_storage_slot,
):
    rows = queries.shape[0]
    replica_rows = rows * lax.axis_size("tensor")
    blocks = block_adapter_index.shape[0]
    block_rows = replica_rows // blocks
    down = jnp.swapaxes(adapter_down_factors, 1, 2)
    up = adapter_up_factors
    if lax.axis_size("tensor") == LINE and block_rows == rows:
        return line_body(
            queries,
            keys,
            values,
            lengths,
            output_projection_weight,
            down,
            up,
            block_adapter_index,
            block_live_rows,
            adapter_storage_slot,
        )
    here, all_ids, packed = pair_factors(down, up, block_adapter_index, adapter_storage_slot)
    paired, merged = merge_factors(here, all_ids, adapter_storage_slot, down, up, packed)
    fetched = fetch_factors(merged)
    attended = lax.all_gather(
        attention(queries, keys, values, lengths), "tensor", axis=0, tiled=True
    )
    order = jnp.arange(blocks, dtype=jnp.int32)
    factors = pick_factors(
        here, all_ids, adapter_storage_slot, order, down, up, paired, fetched
    )
    depth = down.shape[2]
    columns = lax.dynamic_slice_in_dim(
        attended, lax.axis_index("tensor") * depth, depth, 1
    ).reshape(blocks, block_rows, depth)
    partial_rank = jnp.einsum(
        "bri,bki->bkr", columns, factors[:, :, :depth], preferred_element_type=jnp.float32
    )
    reduced = sum_over_tensor(partial_rank).astype(jnp.bfloat16)
    base = dot(attended, output_projection_weight)
    delta = jnp.einsum(
        "bkr,bkc->brc", reduced, factors[:, :, depth:], preferred_element_type=jnp.float32
    )
    live = (jnp.arange(block_rows)[None, :] < block_live_rows[:, None])[..., None]
    base = base.reshape(delta.shape)
    return (
        jnp.where(live, base + 2.0 * delta, 0.0)
        .astype(jnp.bfloat16)
        .reshape(replica_rows, base.shape[2])
    )


def solution(mesh):
    placed = (
        P(("groups", "replica", "tensor"), None),
        P(("groups", "replica", "tensor"), None, None),
        P(("groups", "replica", "tensor"), None, None),
        P(("groups", "replica", "tensor")),
        P(None, "tensor"),
        P(("groups", "replica"), "tensor", None),
        P(("groups", "replica"), None, "tensor"),
        P(("groups", "replica")),
        P(("groups", "replica")),
        P("groups"),
    )
    return jax.shard_map(
        body,
        mesh=mesh,
        in_specs=placed,
        out_specs=P(("groups", "replica"), "tensor"),
        check_vma=False,
    )
```
